512 devices in a mesh: dp: 32 (over x, z_lo, core), fsdp: 2 (over z_hi), tensor: 8 (over y).
Axes of the slice: x: 4, y: 8, z: 8 (z_hi: 2, z_lo: 4; z = z_hi * 4 + z_lo), core: 2. Of those that a mesh axis runs over, the one named last changes fastest.
Arguments:
- hidden: bfloat16 [16384, 4096], P(('dp', 'fsdp')), may hold values from -6 to 6
- lengths: int32 [64], P(('dp', 'fsdp')), may hold values from 64 to 256, as said below
- projection: bfloat16 [4096, 18560], P(('dp', 'fsdp', 'tensor')), may hold values from -0.09375 to 0.09375
- input_gain: float32 [4096], replicated, may hold values from 0.1 to 1.9
- x_kernel: float32 [4, 8192], P(None, 'tensor'), may hold values from -3 to 3
- x_offset: float32 [8192], P('tensor'), may hold values from -3 to 3
- bc_kernel: float32 [4, 2, 1024], P(None, None, 'tensor'), may hold values from -3 to 3
- bc_offset: float32 [2, 1024], P(None, 'tensor'), may hold values from -3 to 3
- step_bias: float32 [128], P('tensor'), may hold values from -5 to -1
- decay_log: float32 [128], P('tensor'), may hold values from -3 to 0.5
- skip_gain: float32 [128], P('tensor'), may hold values from 0.5 to 1.5
- norm_gain: float32 [8192], P('tensor'), may hold values from 0.1 to 1.9
Outputs:
- mixer_out: bfloat16 [16384, 8192], P(('dp', 'fsdp'), 'tensor')
- final_state: float32 [64, 128, 64, 128], P(('dp', 'fsdp'), 'tensor')
The draws below stay inside these ranges and needn't reach their ends.
Inputs may be any that keep to these rules, and one draw needn't show every extreme that they name: `lengths`: each sequence's valid tokens start at the stretch's first position; some sequence fills the whole stretch.
All inputs are finite; a program needn't handle non-finite values.
Results may differ from the reference program's by a relative error of at most 0.04.
Values may be sent and summed in bfloat16 or wider, within the bound.
No kernel may reach another device: no remote copies, remote signals or barrier semaphores. Data moves between devices by JAX's collectives and lax.ppermute only.
A program may use at most 64 MiB of HBM per device.

```python
import jax
import jax.numpy as jnp
from jax import lax

D = 4096
H = 128
P_SIZE = 64
G = 8
N = 128
KC = 4
STRETCH = 256
DI = 8192
PROJ = 18560
SEQS = 64
TOKENS = 16384
N_DP = 32
N_FSDP = 2


def draw_lengths(key, part):
    key = jax.random.fold_in(key, 11)
    first_key, second_key = jax.random.split(key)
    values = jax.random.randint(first_key, (SEQS,), STRETCH // 4, STRETCH + 1)
    chosen = jax.random.randint(second_key, (), 0, SEQS)
    return jnp.where(jnp.arange(SEQS) == chosen, STRETCH, values).astype(jnp.int32)


def shard_levels(key, extent, cuts, least, largest):
    level, own = 1.0, jax.random.fold_in(key, 6)
    for axis_at, blocks in cuts:
        draws = jnp.exp(jax.random.uniform(jax.random.fold_in(own, axis_at), (blocks,), jnp.float32, least / len(cuts), largest / len(cuts)))
        level = level * jnp.repeat(draws, extent[axis_at] // blocks).reshape([-1 if axis == axis_at else 1 for axis in range(len(extent))])
    return level


def bell_draw(own_key, shape, width, reach, cuts=(), kind=jnp.bfloat16):
    result = jax.random.normal(own_key, shape, jnp.float32) * width
    if len(cuts) > 0:
        result = shard_levels(own_key, shape, cuts, -0.22, 0.18) * result
    return jnp.clip(result, min=-reach, max=reach).astype(kind)


def setup_inputs(seed: int = 0) -> dict:
    key_list = jax.random.split(jax.random.key(seed), 13)
    hidden = bell_draw(key_list[0], (TOKENS, D), 1.0, 6.0, ((0, 64),))
    lengths = draw_lengths(jax.random.fold_in(key_list[12], 71), 0)
    projection = bell_draw(key_list[2], (D, PROJ), D ** -0.5, 0.09375, ((0, 512),))
    input_gain = jnp.clip(1.0 + 0.18 * jax.random.normal(key_list[3], (D,), jnp.float32), 0.1, 1.9)
    x_kernel = bell_draw(key_list[4], (KC, DI), KC ** -0.5, 3.0, ((1, 8),), jnp.float32)
    x_offset = bell_draw(key_list[5], (DI,), 0.5, 3.0, ((0, 8),), jnp.float32)
    bc_kernel = bell_draw(key_list[6], (KC, 2, G * N), KC ** -0.5, 3.0, ((2, 8),), jnp.float32)
    bc_offset = bell_draw(key_list[7], (2, G * N), 0.5, 3.0, ((1, 8),), jnp.float32)
    step_bias = jnp.clip(-5.0 + 4.0 * jax.random.uniform(key_list[8], (H,), jnp.float32) ** shard_levels(key_list[8], (H,), ((0, 8),), -0.2, 0.2), -5.0, -1.0)
    decay_log = jnp.clip(-3.0 + 3.5 * jax.random.uniform(key_list[9], (H,), jnp.float32) ** shard_levels(key_list[9], (H,), ((0, 8),), -0.2, 0.2), -3.0, 0.5)
    skip_gain = jnp.clip(0.5 + 1.0 * jax.random.uniform(key_list[10], (H,), jnp.float32) ** shard_levels(key_list[10], (H,), ((0, 8),), -0.2, 0.2), 0.5, 1.5)
    norm_gain = jnp.clip(1.0 + 0.18 * jax.random.normal(key_list[11], (DI,), jnp.float32), 0.1, 1.9)
    return dict(hidden=hidden, lengths=lengths, projection=projection, input_gain=input_gain, x_kernel=x_kernel, x_offset=x_offset, bc_kernel=bc_kernel, bc_offset=bc_offset, step_bias=step_bias, decay_log=decay_log, skip_gain=skip_gain, norm_gain=norm_gain)


EPSILON = 1e-05

def causal_conv(values, kernel, offset):
    tap_count = kernel.shape[0]
    length = values.shape[1]
    pad_shape = [(0, 0), (tap_count - 1, 0)] + [(0, 0)] * (values.ndim - 2)
    padded = jnp.pad(values, pad_shape)
    summed = jnp.zeros_like(values) + offset
    for tap_index in range(tap_count):
        summed = summed + kernel[tap_index] * padded[:, tap_index:tap_index + length]
    return summed

def mamba_core(projected, seq_lengths, x_kernel, x_offset, bc_kernel, bc_offset, step_bias, decay_log, skip_gain, head_count, group_count):
    seq_count = projected.shape[0]
    length = projected.shape[1]
    inner_width = x_kernel.shape[1]
    head_width = inner_width // head_count
    bc_width = bc_kernel.shape[2]
    state_width = bc_width // group_count
    repeat_count = head_count // group_count
    gate_cols = projected[:, :, :inner_width]
    x_cols = projected[:, :, inner_width:2 * inner_width]
    bc_cols = projected[:, :, 2 * inner_width:2 * inner_width + 2 * bc_width].reshape(seq_count, length, 2, bc_width)
    step_raw = projected[:, :, 2 * inner_width + 2 * bc_width:]
    x_active = jax.nn.silu(causal_conv(x_cols, x_kernel, x_offset)).astype(jnp.bfloat16)
    bc_active = jax.nn.silu(causal_conv(bc_cols, bc_kernel, bc_offset)).astype(jnp.bfloat16)
    position = jnp.arange(length, dtype=jnp.int32)
    live_rows = (position[None, :] < seq_lengths[:, None]).astype(jnp.float32)
    step_size = jax.nn.softplus(step_raw + step_bias) * live_rows[:, :, None]
    decay_sum = jnp.cumsum(-jnp.exp(decay_log) * step_size, axis=1)
    decay_heads = jnp.transpose(decay_sum, (0, 2, 1))
    step_heads = jnp.transpose(step_size, (0, 2, 1))
    b_active = bc_active[:, :, 0].reshape(seq_count, length, group_count, state_width)
    c_active = bc_active[:, :, 1].reshape(seq_count, length, group_count, state_width)
    scores = jnp.einsum('stgn,sugn->sgtu', c_active.astype(jnp.float32), b_active.astype(jnp.float32))
    scores = jnp.repeat(scores, repeat_count, axis=1)
    causal = position[:, None] >= position[None, :]
    spread = jnp.where(causal, decay_heads[:, :, :, None] - decay_heads[:, :, None, :], 0.0)
    decays = jnp.where(causal, jnp.exp(spread), 0.0)
    mixing = (scores * decays * step_heads[:, :, None, :]).astype(jnp.bfloat16)
    x_heads = x_active.reshape(seq_count, length, head_count, head_width)
    output = jnp.einsum('shtu,suhp->sthp', mixing.astype(jnp.float32), x_heads.astype(jnp.float32))
    output = output + skip_gain[:, None] * x_heads.astype(jnp.float32)
    gated_out = output.reshape(seq_count, length, inner_width) * jax.nn.silu(gate_cols)
    remaining = jnp.exp(decay_sum[:, -1:, :] - decay_sum) * step_size
    weighted = x_heads.astype(jnp.float32) * remaining[:, :, :, None]
    b_heads = jnp.repeat(b_active, repeat_count, axis=2).astype(jnp.float32)
    final_state = jnp.einsum('suhp,suhn->shpn', weighted, b_heads, precision=lax.Precision.HIGHEST)
    return (gated_out, final_state, live_rows)

def normalize_gated(gated_out, gain, group_count, live_rows):
    seq_count = gated_out.shape[0]
    length = gated_out.shape[1]
    inner_width = gated_out.shape[2]
    grouped = gated_out.reshape(seq_count, length, group_count, inner_width // group_count)
    inverse_rms = lax.rsqrt(lax.optimization_barrier(jnp.mean(grouped * grouped, axis=-1, keepdims=True)) + EPSILON)
    scaled = (grouped * inverse_rms).reshape(seq_count, length, inner_width) * gain
    return (scaled * live_rows[:, :, None]).astype(jnp.bfloat16)

def reference(hidden, lengths, projection, input_gain, x_kernel, x_offset, bc_kernel, bc_offset, step_bias, decay_log, skip_gain, norm_gain):
    block_rows = D // (N_DP * N_FSDP)
    halves = projection.reshape(N_DP, N_FSDP, block_rows, PROJ)
    half_weights = [halves[:, half_index].reshape(N_DP * block_rows, PROJ) for half_index in range(N_FSDP)]

    def one_sequence(packed):
        seq_rows, seq_length = packed
        widened = seq_rows.astype(jnp.float32)
        normed = (widened * lax.rsqrt(lax.optimization_barrier(jnp.mean(widened * widened, axis=-1, keepdims=True)) + EPSILON) * input_gain).astype(jnp.bfloat16)
        viewed = normed.reshape(STRETCH, N_DP, N_FSDP, block_rows)
        projected = jnp.zeros((STRETCH, PROJ), jnp.float32)
        for half_index in range(N_FSDP):
            partial_sum = jnp.dot(viewed[:, :, half_index].reshape(STRETCH, N_DP * block_rows), half_weights[half_index], preferred_element_type=jnp.float32)
            rounded = lax.optimization_barrier(partial_sum.astype(jnp.bfloat16))
            projected = projected + rounded.astype(jnp.float32)
        gated_out, final_state, live_rows = mamba_core(projected[None], seq_length[None], x_kernel, x_offset, bc_kernel, bc_offset, step_bias, decay_log, skip_gain, H, G)
        return (normalize_gated(gated_out, norm_gain, G, live_rows)[0], final_state[0])
    mixed_rows, states = lax.map(one_sequence, (hidden.reshape(SEQS, STRETCH, D), lengths))
    return (mixed_rows.reshape(TOKENS, H * P_SIZE), states)
```

```python
import functools

import jax
import jax.numpy as jnp
from jax import lax
from jax.experimental import pallas as pl
from jax.experimental.pallas import tpu as pltpu
from jax.sharding import Mesh, PartitionSpec as P

EPSILON = 1e-05
F32 = jnp.float32
BF16 = jnp.bfloat16

TOK = 256
D = 4096
QUARTER = 256
NST = 128
HEADS = 4
XC = QUARTER + NST
COLS = XC + QUARTER
WIDE = XC + 128
DEPTH = 512
DZ_ORDER = (0, 1, 7, 2, 6, 3, 5, 4)
DZ_AT = {dz: at for at, dz in enumerate(DZ_ORDER)}

VMEM = pl.BlockSpec(memory_space=pltpu.VMEM)
SMEM = pl.BlockSpec(memory_space=pltpu.SMEM)


def params(mib):
    return pltpu.CompilerParams(vmem_limit_bytes=mib << 20)


def cost(flops, nbytes):
    return pl.CostEstimate(flops=flops, bytes_accessed=nbytes, transcendentals=0)


def silu(value):
    return value * jax.nn.sigmoid(value)


def norm_kernel(at_ref, hidden_ref, gain_ref, out_ref, scale_ref):
    z_at = at_ref[0]
    for rows in range(0, TOK, 32):
        wide = hidden_ref[rows : rows + 32, :].astype(F32)
        mean = jnp.sum(wide * wide, axis=1, keepdims=True) * (1.0 / D)
        scale_ref[rows : rows + 32, :] = jnp.broadcast_to(lax.rsqrt(mean + EPSILON), (32, 128))
    low = lax.broadcasted_iota(jnp.int32, (TOK, 128), 1) < 64
    scale = scale_ref[...]
    for dz in range(4):
        zs = lax.rem(z_at + dz, 8)
        zl = lax.rem(zs, 4)
        here_first = zs < 4
        here = DZ_AT[dz] * DEPTH
        there = DZ_AT[dz + 4] * DEPTH
        here_at = pl.multiple_of(jnp.where(here_first, here, there), 128)
        there_at = pl.multiple_of(jnp.where(here_first, there, here), 128)
        for x in range(4):
            base = pl.multiple_of((x * 4 + zl) * 256, 256)
            second_at = pl.multiple_of(base + 128, 128)
            first = hidden_ref[:, pl.ds(base, 128)].astype(F32) * scale * gain_ref[:, pl.ds(base, 128)]
            second = (
                hidden_ref[:, pl.ds(second_at, 128)].astype(F32)
                * scale
                * gain_ref[:, pl.ds(second_at, 128)]
            )
            low_half = jnp.where(low, first, pltpu.roll(second, 64, 1)).astype(BF16)
            high_half = jnp.where(low, pltpu.roll(first, 64, 1), second).astype(BF16)
            out_ref[:, pl.ds(pl.multiple_of(here_at + x * 128, 128), 128)] = low_half
            out_ref[:, pl.ds(pl.multiple_of(there_at + x * 128, 128), 128)] = high_half


def norm_call(at, hidden, gain):
    return pl.pallas_call(
        norm_kernel,
        out_shape=jax.ShapeDtypeStruct((TOK, D), BF16),
        in_specs=[SMEM, VMEM, VMEM],
        out_specs=VMEM,
        scratch_shapes=[pltpu.VMEM((TOK, 128), F32)],
        compiler_params=params(32),
        cost_estimate=cost(TOK * D * 8, TOK * D * 4),
        name="norm",
    )(at, hidden, gain)


def pieces(weight_refs, plan):
    for weight_ref, (at, depth, steps) in zip(weight_refs, plan):
        yield at, depth, weight_ref, steps


def step_columns(weight_ref, depth):
    tile = weight_ref[depth : depth + 16, :256].astype(F32)
    halves = []
    for half in range(2):
        rows = jnp.concatenate([tile[half * 8 : half * 8 + 8], jnp.zeros((120, 256), F32)], axis=0)
        halves.append(rows.T.astype(BF16))
    return jnp.concatenate(halves, axis=0)


def add_to(total, part):
    return part if total is None else total + part


def products(hidden_refs, weight_refs, plan, lanes, with_steps, use):
    tails = {}
    if with_steps:
        tails = {i: step_columns(w, d) for i, (_, d, w, s) in enumerate(pieces(weight_refs, plan)) if s}
    for seq, hidden_ref in enumerate(hidden_refs):
        total, steps = None, None
        for i, (at, depth, weight_ref, _) in enumerate(pieces(weight_refs, plan)):
            left = hidden_ref[:, at : at + depth]
            right = weight_ref[:depth, lanes]
            total = add_to(total, jnp.dot(left, right, preferred_element_type=F32))
            if i in tails:
                first = at // DEPTH * DEPTH
                left = hidden_ref[:, first : first + DEPTH]
                steps = add_to(steps, jnp.dot(left, tails[i], preferred_element_type=F32))
        use(seq, total, steps)


def plan_of(*dzs):
    return tuple((DZ_AT[dz] * DEPTH, DEPTH, True) for dz in dzs)


def pair_kernel(plan, has_total, keep_last, *refs):
    weight_refs = refs[2 : 2 + len(plan)]
    before_ref = refs[2 + len(plan)]
    out_ref = refs[-2 if keep_last else -1]

    def use(seq, total, steps):
        rows = pl.ds(seq * TOK, TOK)
        for lanes, part in (
            (slice(0, XC), total[:, :XC]),
            (slice(XC, WIDE), steps),
            (slice(WIDE, WIDE + QUARTER), total[:, XC:]),
        ):
            out_ref[rows, lanes] = part + before_ref[rows, lanes] if has_total else part
        if keep_last:
            refs[-1][rows, :] = refs[seq][:, DZ_AT[4] * DEPTH :]

    products(refs[:2], weight_refs, plan, slice(None), True, use)


def pair_call(hiddens, weights, plan, total, name):
    keep_last = total is not None
    operands = [*hiddens, *weights] + ([total] if keep_last else [])
    shapes = [jax.ShapeDtypeStruct((2 * TOK, WIDE + QUARTER), F32)]
    if keep_last:
        shapes.append(jax.ShapeDtypeStruct((2 * TOK, DEPTH), BF16))
    return pl.pallas_call(
        functools.partial(pair_kernel, plan, keep_last, keep_last),
        out_shape=tuple(shapes),
        in_specs=[VMEM] * len(operands),
        out_specs=(VMEM,) * len(shapes),
        compiler_params=params(48),
        cost_estimate=cost(8 * TOK * DEPTH * len(plan) * (WIDE + QUARTER), 8 * TOK * D),
        name=name,
    )(*operands)


def shifted(value, by):
    row = lax.broadcasted_iota(jnp.int32, value.shape, 0)
    return jnp.where(row < by, 0.0, pltpu.roll(value, by, 0))


def causal_conv(value, taps, offset):
    total = offset + taps[0] * shifted(value, 3)
    total = total + taps[1] * shifted(value, 2)
    total = total + taps[2] * shifted(value, 1)
    return total + taps[3] * value


def last_kernel(plan, at_ref, *refs):
    totals, weight_refs = refs[2:4], refs[4 : 4 + len(plan)]
    kernel_ref, offset_ref, x_ref, bc_ref, steps_ref, gate_ref = refs[4 + len(plan) :]
    core = at_ref[1]
    taps = [kernel_ref[tap, pl.ds(core, 1), :] for tap in range(4)]
    offset = offset_ref[pl.ds(core, 1), :]

    def use(seq, total, steps):
        rows = pl.ds(seq * TOK, TOK)
        before = pl.ds(seq % 2 * TOK, TOK)
        total_ref = totals[seq // 2]
        x_ref[rows, :] = total[:, :QUARTER] + total_ref[before, :QUARTER]
        bc = total[:, QUARTER:XC] + total_ref[before, QUARTER:XC]
        bc_ref[rows, :] = silu(causal_conv(bc, taps, offset)).astype(BF16)
        steps_ref[rows, :] = steps + total_ref[before, XC:WIDE]
        gate_ref[rows, :] = silu(total[:, XC:] + total_ref[before, WIDE:])

    hidden_refs = [refs[seq // 2].at[pl.ds(seq % 2 * TOK, TOK), :] for seq in range(4)]
    products(hidden_refs, weight_refs, plan, slice(None), True, use)


def last_call(at, hiddens, totals, weights, plan, bc_kernel, bc_offset):
    return pl.pallas_call(
        functools.partial(last_kernel, plan),
        out_shape=(
            jax.ShapeDtypeStruct((4 * TOK, QUARTER), F32),
            jax.ShapeDtypeStruct((4 * TOK, NST), BF16),
            jax.ShapeDtypeStruct((4 * TOK, 128), F32),
            jax.ShapeDtypeStruct((4 * TOK, QUARTER), F32),
        ),
        in_specs=[SMEM] + [VMEM] * (6 + len(weights)),
        out_specs=(VMEM,) * 4,
        compiler_params=params(40),
        cost_estimate=cost(8 * TOK * DEPTH * (WIDE + QUARTER), 8 * TOK * WIDE),
        name="last",
    )(at, *hiddens, *totals, *weights, bc_kernel, bc_offset)


def core_kernel(
    seq,
    at_ref,
    skip_ref,
    bias_ref,
    decay_ref,
    length_ref,
    gate_ref,
    x_ref,
    bc_own_ref,
    bc_other_ref,
    step_ref,
    x_kernel_ref,
    x_offset_ref,
    *out_refs,
):
    core = at_ref[1]
    group = at_ref[2] * 2 + core
    units = pl.ds(pl.multiple_of(group * QUARTER, QUARTER), QUARTER)
    mine = core == 0
    b_act = jnp.where(mine, bc_own_ref[...], bc_other_ref[...])
    c_act = jnp.where(mine, bc_other_ref[...], bc_own_ref[...])
    x_taps = [x_kernel_ref[tap : tap + 1, units] for tap in range(4)]
    x_act = silu(causal_conv(x_ref[...], x_taps, x_offset_ref[:, units])).astype(BF16)
    x_wide = x_act.astype(F32)

    head_at = lax.broadcasted_iota(jnp.int32, (8, TOK), 0)
    bias = jnp.zeros((8, TOK), F32)
    decay = jnp.zeros((8, TOK), F32)
    for head in range(HEADS):
        bias = jnp.where(head_at == head, bias_ref[group * HEADS + head], bias)
        decay = jnp.where(head_at == head, decay_ref[group * HEADS + head], decay)
    length = length_ref[jnp.bitwise_xor(group, seq)]
    live = lax.broadcasted_iota(jnp.int32, (8, TOK), 1).astype(F32) < length
    raw = step_ref[...].T[:8] + bias
    soft = jnp.maximum(raw, 0.0) + jnp.log1p(jnp.exp(-jnp.abs(raw)))
    step = jnp.where(live, soft, 0.0)
    ends = -jnp.exp(decay) * step
    row = lax.broadcasted_iota(jnp.int32, (TOK, TOK), 0)
    col = lax.broadcasted_iota(jnp.int32, (TOK, TOK), 1)
    ones = jnp.where(row <= col, 1.0, 0.0).astype(F32)
    sums = jnp.dot(ends, ones, precision=lax.Precision.HIGHEST, preferred_element_type=F32)
    left_over = jnp.exp(sums[:, TOK - 1 :] - sums) * step
    packed = jnp.concatenate([sums, left_over, jnp.zeros((112, TOK), F32)], axis=0)
    columns = packed.T

    scores = lax.dot_general(c_act, b_act, (((1,), (1,)), ((), ())), preferred_element_type=F32)
    causal = row >= col
    low = lax.broadcasted_iota(jnp.int32, (TOK, 128), 1) < 64
    outs, weighted = [], []
    for pair in range(HEADS // 2):
        lanes = slice(pair * 128, pair * 128 + 128)
        halves = []
        for head in (2 * pair, 2 * pair + 1):
            spread = jnp.where(causal, columns[:, head : head + 1] - sums[head : head + 1, :], -1e30)
            mixing = (scores * jnp.exp(spread) * step[head : head + 1, :]).astype(BF16)
            halves.append(jnp.dot(mixing, x_act[:, lanes], preferred_element_type=F32))
        skip = jnp.where(
            low[:1], skip_ref[group * HEADS + 2 * pair], skip_ref[group * HEADS + 2 * pair + 1]
        )
        outs.append(jnp.where(low, halves[0], halves[1]) + skip * x_wide[:, lanes])
        at = 8 + 2 * pair
        weighted.append(
            x_wide[:, lanes] * jnp.where(low, columns[:, at : at + 1], columns[:, at + 1 : at + 2])
        )
    gated = jnp.concatenate(outs, axis=1) * gate_ref[...]
    spread_x = jnp.concatenate(weighted, axis=1)
    state = jnp.dot(spread_x.T.astype(BF16), b_act, preferred_element_type=F32)
    if seq == 0:
        out_refs[0][...] = gated
        out_refs[1][...] = state
    else:
        out_refs[0][:, :QUARTER] = gated.astype(BF16)
        out_refs[0][:, QUARTER:] = state.astype(BF16)


def core_call(seq, at, skip, bias, decay, lengths, gate, x_cols, bc_own, bc_other, steps, x_kernel, x_offset):
    if seq == 0:
        out_shape = (
            jax.ShapeDtypeStruct((TOK, QUARTER), F32),
            jax.ShapeDtypeStruct((QUARTER, NST), F32),
        )
    else:
        out_shape = (jax.ShapeDtypeStruct((TOK, QUARTER + NST), BF16),)

    def rows(at_block, width):
        return pl.BlockSpec((TOK, width), lambda i: (at_block, 0))

    def whole(array):
        return pl.BlockSpec(array.shape, lambda i: (0,) * array.ndim)

    return pl.pallas_call(
        functools.partial(core_kernel, seq),
        grid=(1,),
        out_shape=out_shape,
        in_specs=[
            SMEM,
            SMEM,
            SMEM,
            SMEM,
            SMEM,
            rows(seq, QUARTER),
            rows(seq, QUARTER),
            rows(seq, NST),
            rows(seq ^ 1, NST),
            rows(seq, 128),
            whole(x_kernel),
            whole(x_offset),
        ],
        out_specs=tuple(pl.BlockSpec(s.shape, lambda i: (0, 0)) for s in out_shape),
        compiler_params=params(32),
        cost_estimate=cost(8 * TOK * TOK * 200, 8 * TOK * QUARTER),
        name=("core_own", "core_other", "core_x", "core_far")[seq],
    )(at, skip, bias, decay, lengths, gate, x_cols, bc_own, bc_other, steps, x_kernel, x_offset)


def final_kernel(at_ref, length_ref, own_ref, state_ref, a_ref, b_ref, c_ref, gain_ref, out_ref, final_ref):
    group = at_ref[2] * 2 + at_ref[1]
    own = own_ref[...]
    squares = jnp.sum(own * own, axis=1, keepdims=True)
    parts = [(0, own)]
    for flip, ref in ((1, a_ref), (2, b_ref), (3, c_ref)):
        part = ref[:, :QUARTER].astype(F32)
        squares = squares + jnp.sum(part * part, axis=1, keepdims=True)
        parts.append((flip, part))
    live = lax.broadcasted_iota(jnp.int32, (TOK, 1), 0) < length_ref[0]
    scale = jnp.where(live, lax.rsqrt(squares * (1.0 / (4 * QUARTER)) + EPSILON), 0.0)
    for flip, part in parts:
        at = pl.ds(pl.multiple_of(jnp.bitwise_xor(group, flip) * QUARTER, QUARTER), QUARTER)
        out_ref[:, at] = (part * scale * gain_ref[:, at]).astype(BF16)
        if flip == 0:
            final_ref[at, :] = state_ref[...]
        else:
            final_ref[at, :] = (a_ref, b_ref, c_ref)[flip - 1][:, QUARTER:].astype(F32)


def final_call(at, length, own, state, got, gain):
    return pl.pallas_call(
        final_kernel,
        out_shape=(
            jax.ShapeDtypeStruct((TOK, 4 * QUARTER), BF16),
            jax.ShapeDtypeStruct((4 * QUARTER, NST), F32),
        ),
        in_specs=[SMEM, SMEM] + [VMEM] * 6,
        out_specs=(VMEM, VMEM),
        compiler_params=params(32),
        cost_estimate=cost(TOK * QUARTER * 40, TOK * QUARTER * 32),
        name="gated_norm",
    )(at, length, own, state, *got, gain)


def from_z(value, distance):
    flat = lambda z: (z % 4) * 2 + z // 4
    return lax.ppermute(
        value, ("zl", "zh"), [(flat((i + distance) % 8), flat(i)) for i in range(8)]
    )


def swap_core(value):
    return lax.ppermute(value, "core", [(0, 1), (1, 0)])


def swap_x(value):
    return lax.ppermute(value, "xb", [(0, 1), (1, 0)])


def swap_both(value):
    return lax.ppermute(value, ("xb", "core"), [(0, 3), (1, 2), (2, 1), (3, 0)])


def device_slices(projection, length):
    inner = 32 * QUARTER
    gate, x_cols = (
        projection[:, at : at + inner].reshape(8, 8, 2, 2, QUARTER).transpose(0, 2, 3, 1, 4)
        for at in (0, inner)
    )
    bc = projection[:, 2 * inner : 2 * inner + 2048].reshape(8, 1, 2, 8, NST)
    steps = projection[:, 2 * inner + 2048 :].reshape(8, 8, 2, 2, HEADS).transpose(0, 2, 3, 1, 4)
    length = jnp.broadcast_to(length.astype(BF16), (8, 2, 2, 8, 1))
    joined = jnp.concatenate(
        [x_cols, jnp.broadcast_to(bc, (8, 2, 2, 8, NST)), gate, steps, length], axis=4
    )
    width = joined.shape[4]
    return jnp.broadcast_to(joined[:, None], (8, 2, 2, 2, 8, width)).reshape(8, 64, width)


def on_device(
    hidden,
    lengths,
    projection,
    input_gain,
    x_kernel,
    x_offset,
    bc_kernel,
    bc_offset,
    step_bias,
    decay_log,
    skip_gain,
    norm_gain,
):
    z_at = lax.axis_index("zh") * 4 + lax.axis_index("zl")
    at = jnp.stack([z_at, lax.axis_index("core"), lax.axis_index("xb")])
    gain = input_gain.reshape(1, D)

    block = lax.all_to_all(
        device_slices(projection, lengths),
        ("xa", "xb", "core", "y"),
        split_axis=1,
        concat_axis=0,
        tiled=True,
    ).reshape(DEPTH, COLS + HEADS + 1)
    own = norm_call(at, hidden, gain)
    block, own = lax.optimization_barrier((block, own))

    step_rows = jnp.pad(block[:, COLS : COLS + HEADS].T, ((0, 4), (0, 0)))
    step_rows = jnp.concatenate([step_rows[:, :256], step_rows[:, 256:]], axis=0)
    w0 = jnp.concatenate(
        [block[:, :COLS], jnp.pad(step_rows, ((0, 0), (0, COLS - 256)))], axis=0
    )
    lengths_all = block[:, COLS + HEADS].reshape(2, 4, 64)
    lengths_all = lax.dynamic_index_in_dim(lengths_all, lax.axis_index("xa"), 0, keepdims=False)
    lengths_all = lax.dynamic_index_in_dim(lengths_all, lax.axis_index("y") * 8, 1, keepdims=False)
    lengths_all = lengths_all.astype(F32)
    w1, w7 = from_z(w0, 1), from_z(w0, -1)
    own_x = swap_x(own)
    other = swap_core(own)
    w2, w6 = from_z(w1, 1), from_z(w7, -1)
    w2, w6, own_x = lax.optimization_barrier((w2, w6, own_x))
    far = swap_core(own_x)
    w3, w5 = from_z(w2, 1), from_z(w6, -1)

    near = pair_call([own, other], [w0, w1, w7, w2, w6], plan_of(0, 1, 7, 2, 6), None, "near")[0]
    w3, w5, near, lengths_all = lax.optimization_barrier((w3, w5, near, lengths_all))
    w4a, w4b = from_z(w3[:256], 1), from_z(w5[256:], -1)
    away = pair_call([own_x, far], [w0, w1, w7, w2, w6], plan_of(0, 1, 7, 2, 6), None, "away")[0]
    near, near_last = pair_call([own, other], [w3, w5], plan_of(3, 5), near, "near_late")
    away, away_last = pair_call([own_x, far], [w3, w5], plan_of(3, 5), away, "away_late")
    last = ((0, 256, False), (256, 256, True))
    lasts, totals, weights = (near_last, away_last), (near, away), (w4a, w4b)
    x_cols, bc_own, steps, gate = last_call(
        at, lasts, totals, weights, last, bc_kernel, bc_offset
    )
    bc_other = swap_core(bc_own)
    arguments = (
        gate,
        x_cols,
        bc_own,
        bc_other,
        steps,
        x_kernel,
        x_offset.reshape(1, 4 * QUARTER),
    )

    def core(seq):
        return core_call(seq, at, skip_gain, step_bias, decay_log, lengths_all, *arguments)

    sent = core(3)[0]
    arguments, sent = lax.optimization_barrier((arguments, sent))
    got_far = swap_both(sent)
    sent = core(2)[0]
    arguments, sent = lax.optimization_barrier((arguments, sent))
    got_x = swap_x(sent)
    sent = core(1)[0]
    arguments, sent = lax.optimization_barrier((arguments, sent))
    got_other = swap_core(sent)
    gated, state = core(0)
    mixer_out, final_state = final_call(
        at, lengths, gated, state, (got_other, got_x, got_far), norm_gain.reshape(1, 4 * QUARTER)
    )
    return mixer_out, final_state.reshape(1, 4 * HEADS, QUARTER // HEADS, NST)


def solution(mesh):
    names = ("xa", "xb", "zl", "core", "zh", "y")
    fine = Mesh(mesh.devices.reshape(2, 2, 4, 2, 2, 8), names)
    replica = names[:5]
    in_specs = (
        P(replica, None),
        P(replica),
        P(names, None),
        P(),
        P(None, "y"),
        P("y"),
        P(None, None, "y"),
        P(None, "y"),
        P("y"),
        P("y"),
        P("y"),
        P("y"),
    )
    out_specs = (P(replica, "y"), P(replica, "y", None, None))
    return jax.shard_map(
        on_device, mesh=fine, in_specs=in_specs, out_specs=out_specs, check_vma=False
    )
```

```python
import functools

import jax
import jax.numpy as jnp
from jax import lax
from jax.experimental import pallas as pl
from jax.experimental.pallas import tpu as pltpu
from jax.sharding import Mesh, PartitionSpec as P

EPSILON = 1e-05
F32 = jnp.float32
BF16 = jnp.bfloat16

TOK = 256
D = 4096
QUARTER = 256
NST = 128
HEADS = 4
XC = QUARTER + NST
COLS = XC + QUARTER
WIDE = XC + 128
HALF = 256
DEPTH = 2 * HALF
PACKED = DEPTH + 16
SENT = 768
DZ_ORDER = (0, 1, 7, 2, 6, 3, 5, 4)
DZ_AT = {dz: at for at, dz in enumerate(DZ_ORDER)}

VMEM = pl.BlockSpec(memory_space=pltpu.VMEM)
SMEM = pl.BlockSpec(memory_space=pltpu.SMEM)


def params(mib):
    return pltpu.CompilerParams(vmem_limit_bytes=mib << 20)


def cost(flops, nbytes):
    return pl.CostEstimate(flops=flops, bytes_accessed=nbytes, transcendentals=0)


def silu(value):
    return value * jax.nn.sigmoid(value)


def norm_kernel(at_ref, hidden_ref, gain_ref, out_ref, scale_ref):
    z_at = at_ref[0]
    for rows in range(0, TOK, 32):
        wide = hidden_ref[rows : rows + 32, :].astype(F32)
        mean = jnp.sum(wide * wide, axis=1, keepdims=True) * (1.0 / D)
        scale_ref[rows : rows + 32, :] = jnp.broadcast_to(lax.rsqrt(mean + EPSILON), (32, 128))
    low = lax.broadcasted_iota(jnp.int32, (TOK, 128), 1) < 64
    scale = scale_ref[...]
    for dz in range(4):
        zs = lax.rem(z_at + dz, 8)
        zl = lax.rem(zs, 4)
        here_first = zs < 4
        here = DZ_AT[dz] * DEPTH
        there = DZ_AT[dz + 4] * DEPTH
        here_at = pl.multiple_of(jnp.where(here_first, here, there), 128)
        there_at = pl.multiple_of(jnp.where(here_first, there, here), 128)
        for part in range(4):
            base = pl.multiple_of((part * 4 + zl) * 256, 256)
            second_at = pl.multiple_of(base + 128, 128)
            first = hidden_ref[:, pl.ds(base, 128)].astype(F32) * scale * gain_ref[:, pl.ds(base, 128)]
            second = (
                hidden_ref[:, pl.ds(second_at, 128)].astype(F32)
                * scale
                * gain_ref[:, pl.ds(second_at, 128)]
            )
            low_half = jnp.where(low, first, pltpu.roll(second, 64, 1)).astype(BF16)
            high_half = jnp.where(low, pltpu.roll(first, 64, 1), second).astype(BF16)
            out_ref[:, pl.ds(pl.multiple_of(here_at + part * 128, 128), 128)] = low_half
            out_ref[:, pl.ds(pl.multiple_of(there_at + part * 128, 128), 128)] = high_half


def norm_call(at, hidden, gain):
    return pl.pallas_call(
        norm_kernel,
        out_shape=jax.ShapeDtypeStruct((TOK, D), BF16),
        in_specs=[SMEM, VMEM, VMEM],
        out_specs=VMEM,
        scratch_shapes=[pltpu.VMEM((TOK, 128), F32)],
        compiler_params=params(32),
        cost_estimate=cost(TOK * D * 8, TOK * D * 4),
        name="norm",
    )(at, hidden, gain)


def cut_kernel(length_ref, rows_ref, out_ref):
    inner = 32 * QUARTER
    lane = lax.broadcasted_iota(jnp.int32, (8, 128), 1)
    length = length_ref[0].astype(F32)
    steps = rows_ref[:, 2 * inner + 2048 :].astype(F32)
    for to in range(32):
        group, y = to // 8, to % 8
        units = y * 4 * QUARTER + group * QUARTER
        bc = 2 * inner + (group % 2) * 1024 + y * NST
        at = y * 16 + group * HEADS
        mine = steps if at == 0 else pltpu.roll(steps, 128 - at, 1)
        tail = jnp.where(lane < HEADS, mine, jnp.where(lane == HEADS, length, 0.0))
        for side in (to, to + 32):
            out_ref[side, :, :QUARTER] = rows_ref[:, inner + units : inner + units + QUARTER]
            out_ref[side, :, QUARTER:XC] = rows_ref[:, bc : bc + NST]
            out_ref[side, :, XC:COLS] = rows_ref[:, units : units + QUARTER]
            out_ref[side, :, COLS:] = tail.astype(BF16)


def cut_call(length, rows):
    return pl.pallas_call(
        cut_kernel,
        out_shape=jax.ShapeDtypeStruct((64, 8, SENT), BF16),
        in_specs=[SMEM, VMEM],
        out_specs=VMEM,
        compiler_params=params(32),
        cost_estimate=cost(1000, 1000),
        name="cut",
    )(length, rows)


def pack_kernel(block_ref, out_ref, lengths_ref):
    out_ref[:DEPTH, :] = block_ref[:, :COLS]
    tail = block_ref[:, COLS:].astype(F32).T
    row = lax.broadcasted_iota(jnp.int32, (8, HALF), 0)
    halves = [jnp.where(row < HEADS, tail[:8, at : at + HALF], 0.0) for at in (0, HALF)]
    out_ref[DEPTH:, :HALF] = jnp.concatenate(halves, axis=0).astype(BF16)
    out_ref[DEPTH:, HALF:] = jnp.zeros((16, COLS - HALF), BF16)
    lengths_ref[...] = tail[:8]


def pack_call(block):
    return pl.pallas_call(
        pack_kernel,
        out_shape=(
            jax.ShapeDtypeStruct((PACKED, COLS), BF16),
            jax.ShapeDtypeStruct((8, DEPTH), F32),
        ),
        in_specs=[VMEM],
        out_specs=(VMEM, VMEM),
        compiler_params=params(32),
        cost_estimate=cost(1000, 1000),
        name="pack",
    )(block)


def step_columns(tile):
    wide = jnp.concatenate([tile.astype(F32), jnp.zeros((112, HALF), F32)], axis=0).T
    return [wide.astype(BF16), pltpu.roll(wide, 120, 1).astype(BF16)]


def products(hidden_refs, weight_refs, first, use):
    rows = [ref[: ref.shape[0] // HALF * HALF, :] for ref in weight_refs]
    steps = []
    for ref in weight_refs:
        if ref.shape[0] % HALF:
            steps += step_columns(ref[ref.shape[0] - 16 :, :HALF])
    rows = jnp.concatenate(rows, axis=0)
    steps = jnp.concatenate(steps, axis=0)
    right = jnp.concatenate([rows[:, :XC], steps, rows[:, XC:]], axis=1)
    for seq, ref in enumerate(hidden_refs):
        left = ref[:, first : first + right.shape[0]]
        use(seq, jnp.dot(left, right, preferred_element_type=F32))


def pair_kernel(count, first, has_total, *refs):
    weight_refs = refs[2 : 2 + count]
    out_ref = refs[-2 if has_total else -1]

    def use(seq, part):
        rows = pl.ds(seq * TOK, TOK)
        out_ref[rows, :] = part + refs[2 + count][rows, :] if has_total else part
        if has_total:
            refs[-1][rows, :] = refs[seq][:, DZ_AT[4] * DEPTH :]

    products(refs[:2], weight_refs, first, use)


def pair_call(hiddens, weights, first, total, name):
    operands = [*hiddens, *weights] + ([] if total is None else [total])
    shapes = [jax.ShapeDtypeStruct((2 * TOK, WIDE + QUARTER), F32)]
    if total is not None:
        shapes.append(jax.ShapeDtypeStruct((2 * TOK, DEPTH), BF16))
    return pl.pallas_call(
        functools.partial(pair_kernel, len(weights), first, total is not None),
        out_shape=tuple(shapes),
        in_specs=[VMEM] * len(operands),
        out_specs=(VMEM,) * len(shapes),
        compiler_params=params(48),
        cost_estimate=cost(4 * TOK * DEPTH * len(weights) * (WIDE + QUARTER), 4 * TOK * D),
        name=name,
    )(*operands)


def shifted(value, by):
    row = lax.broadcasted_iota(jnp.int32, value.shape, 0)
    return jnp.where(row < by, 0.0, pltpu.roll(value, by, 0))


def causal_conv(value, taps, offset):
    total = offset + taps[0] * shifted(value, 3)
    total = total + taps[1] * shifted(value, 2)
    total = total + taps[2] * shifted(value, 1)
    return total + taps[3] * value


def last_kernel(count, at_ref, *refs):
    totals, weight_refs = refs[2:4], refs[4 : 4 + count]
    kernel_ref, offset_ref, x_ref, bc_ref, steps_ref, gate_ref = refs[4 + count :]
    core = at_ref[1]
    taps = [kernel_ref[tap, pl.ds(core, 1), :] for tap in range(4)]
    offset = offset_ref[pl.ds(core, 1), :]

    def use(seq, part):
        rows = pl.ds(seq * TOK, TOK)
        part = part + totals[seq // 2][pl.ds(seq % 2 * TOK, TOK), :]
        x_ref[rows, :] = part[:, :QUARTER]
        bc_ref[rows, :] = silu(causal_conv(part[:, QUARTER:XC], taps, offset)).astype(BF16)
        steps_ref[rows, :] = part[:, XC:WIDE]
        gate_ref[rows, :] = silu(part[:, WIDE:])

    hidden_refs = [refs[seq // 2].at[pl.ds(seq % 2 * TOK, TOK), :] for seq in range(4)]
    products(hidden_refs, weight_refs, 0, use)


def last_call(at, hiddens, totals, weights, bc_kernel, bc_offset):
    return pl.pallas_call(
        functools.partial(last_kernel, len(weights)),
        out_shape=(
            jax.ShapeDtypeStruct((4 * TOK, QUARTER), F32),
            jax.ShapeDtypeStruct((4 * TOK, NST), BF16),
            jax.ShapeDtypeStruct((4 * TOK, 128), F32),
            jax.ShapeDtypeStruct((4 * TOK, QUARTER), F32),
        ),
        in_specs=[SMEM] + [VMEM] * (6 + len(weights)),
        out_specs=(VMEM,) * 4,
        compiler_params=params(40),
        cost_estimate=cost(8 * TOK * DEPTH * (WIDE + QUARTER), 8 * TOK * WIDE),
        name="last",
    )(at, *hiddens, *totals, *weights, bc_kernel, bc_offset)


def core_of(seq, refs, out_refs):
    (
        at_ref,
        skip_ref,
        bias_ref,
        decay_ref,
        length_ref,
        gate_ref,
        x_ref,
        bc_own_ref,
        bc_other_ref,
        step_ref,
        x_kernel_ref,
        x_offset_ref,
    ) = refs
    rows = slice(seq * TOK, seq * TOK + TOK)
    turned = slice((seq ^ 1) * TOK, (seq ^ 1) * TOK + TOK)
    core = at_ref[1]
    group = at_ref[2] * 2 + core
    units = pl.ds(pl.multiple_of(group * QUARTER, QUARTER), QUARTER)
    mine = core == 0
    b_act = jnp.where(mine, bc_own_ref[rows, :], bc_other_ref[turned, :])
    c_act = jnp.where(mine, bc_other_ref[turned, :], bc_own_ref[rows, :])
    x_taps = [x_kernel_ref[tap : tap + 1, units] for tap in range(4)]
    x_act = silu(causal_conv(x_ref[rows, :], x_taps, x_offset_ref[:, units])).astype(BF16)
    x_wide = x_act.astype(F32)

    head_at = lax.broadcasted_iota(jnp.int32, (8, TOK), 0)
    bias = jnp.zeros((8, TOK), F32)
    decay = jnp.zeros((8, TOK), F32)
    for head in range(HEADS):
        bias = jnp.where(head_at == head, bias_ref[group * HEADS + head], bias)
        decay = jnp.where(head_at == head, decay_ref[group * HEADS + head], decay)
    holder = ((at_ref[3] * 4 + jnp.bitwise_xor(group, seq)) * 8 + at_ref[4]) * 8
    lane = lax.broadcasted_iota(jnp.int32, (1, DEPTH), 1)
    length = jnp.sum(jnp.where(lane == holder, length_ref[HEADS : HEADS + 1, :], 0.0))
    live = lax.broadcasted_iota(jnp.int32, (8, TOK), 1).astype(F32) < length
    raw = step_ref[rows, :].T[:8] + bias
    soft = jnp.maximum(raw, 0.0) + jnp.log1p(jnp.exp(-jnp.abs(raw)))
    step = jnp.where(live, soft, 0.0)
    ends = -jnp.exp(decay) * step
    row = lax.broadcasted_iota(jnp.int32, (TOK, TOK), 0)
    col = lax.broadcasted_iota(jnp.int32, (TOK, TOK), 1)
    ones = jnp.where(row <= col, 1.0, 0.0).astype(F32)
    sums = jnp.dot(ends, ones, precision=lax.Precision.HIGHEST, preferred_element_type=F32)
    left_over = jnp.exp(sums[:, TOK - 1 :] - sums) * step
    packed = jnp.concatenate([sums, left_over, jnp.zeros((112, TOK), F32)], axis=0)
    columns = packed.T

    scores = lax.dot_general(c_act, b_act, (((1,), (1,)), ((), ())), preferred_element_type=F32)
    causal = row >= col
    low = lax.broadcasted_iota(jnp.int32, (TOK, 128), 1) < 64
    outs, weighted = [], []
    for pair in range(HEADS // 2):
        lanes = slice(pair * 128, pair * 128 + 128)
        halves = []
        for head in (2 * pair, 2 * pair + 1):
            spread = jnp.where(causal, columns[:, head : head + 1] - sums[head : head + 1, :], -1e30)
            mixing = (scores * jnp.exp(spread) * step[head : head + 1, :]).astype(BF16)
            halves.append(jnp.dot(mixing, x_act[:, lanes], preferred_element_type=F32))
        skip = jnp.where(
            low[:1], skip_ref[group * HEADS + 2 * pair], skip_ref[group * HEADS + 2 * pair + 1]
        )
        outs.append(jnp.where(low, halves[0], halves[1]) + skip * x_wide[:, lanes])
        at = 8 + 2 * pair
        weighted.append(
            x_wide[:, lanes] * jnp.where(low, columns[:, at : at + 1], columns[:, at + 1 : at + 2])
        )
    gated = jnp.concatenate(outs, axis=1) * gate_ref[rows, :]
    spread_x = jnp.concatenate(weighted, axis=1)
    state = jnp.dot(spread_x.T.astype(BF16), b_act, preferred_element_type=F32)
    if seq == 0:
        out_refs[0][...] = gated
        out_refs[1][...] = state
    else:
        out_refs[0][:, :QUARTER] = gated.astype(BF16)
        out_refs[0][:, QUARTER:] = state.astype(BF16)


def core_kernel(seqs, *refs):
    for at, seq in enumerate(seqs):
        core_of(seq, refs[:12], refs[12 + at :])


def core_call(seqs, *operands):
    shapes = [jax.ShapeDtypeStruct((TOK, QUARTER + NST), BF16) for seq in seqs if seq]
    if seqs[-1] == 0:
        shapes += [
            jax.ShapeDtypeStruct((TOK, QUARTER), F32),
            jax.ShapeDtypeStruct((QUARTER, NST), F32),
        ]
    return pl.pallas_call(
        functools.partial(core_kernel, seqs),
        out_shape=tuple(shapes),
        in_specs=[SMEM] * 4 + [VMEM] * 8,
        out_specs=(VMEM,) * len(shapes),
        compiler_params=params(40),
        cost_estimate=cost(1000, 1000),
        name="core" + "".join(str(seq) for seq in seqs),
    )(*operands)


def final_kernel(at_ref, length_ref, own_ref, state_ref, c_ref, b_ref, a_ref, gain_ref, out_ref, final_ref):
    group = at_ref[2] * 2 + at_ref[1]
    own = own_ref[...]
    squares = jnp.sum(own * own, axis=1, keepdims=True)
    parts = [(0, own)]
    for flip, ref in ((1, a_ref), (2, b_ref), (3, c_ref)):
        part = ref[:, :QUARTER].astype(F32)
        squares = squares + jnp.sum(part * part, axis=1, keepdims=True)
        parts.append((flip, part))
    live = lax.broadcasted_iota(jnp.int32, (TOK, 1), 0) < length_ref[0]
    scale = jnp.where(live, lax.rsqrt(squares * (1.0 / (4 * QUARTER)) + EPSILON), 0.0)
    for flip, part in parts:
        at = pl.ds(pl.multiple_of(jnp.bitwise_xor(group, flip) * QUARTER, QUARTER), QUARTER)
        out_ref[:, at] = (part * scale * gain_ref[:, at]).astype(BF16)
        if flip == 0:
            final_ref[at, :] = state_ref[...]
        else:
            final_ref[at, :] = (a_ref, b_ref, c_ref)[flip - 1][:, QUARTER:].astype(F32)


def final_call(at, length, own, state, got, gain):
    return pl.pallas_call(
        final_kernel,
        out_shape=(
            jax.ShapeDtypeStruct((TOK, 4 * QUARTER), BF16),
            jax.ShapeDtypeStruct((4 * QUARTER, NST), F32),
        ),
        in_specs=[SMEM, SMEM] + [VMEM] * 6,
        out_specs=(VMEM, VMEM),
        compiler_params=params(32),
        cost_estimate=cost(TOK * QUARTER * 40, TOK * QUARTER * 32),
        name="gated_norm",
    )(at, length, own, state, *got, gain)


def from_z(value, distance):
    flat = lambda z: (z % 4) * 2 + z // 4
    return lax.ppermute(
        value, ("zl", "zh"), [(flat((i + distance) % 8), flat(i)) for i in range(8)]
    )


def swap_core(value):
    return lax.ppermute(value, "core", [(0, 1), (1, 0)])


def swap_x(value):
    return lax.ppermute(value, "xb", [(0, 1), (1, 0)])


def swap_both(value):
    return lax.ppermute(value, ("xb", "core"), [(0, 3), (1, 2), (2, 1), (3, 0)])


def on_device(
    hidden,
    lengths,
    projection,
    input_gain,
    x_kernel,
    x_offset,
    bc_kernel,
    bc_offset,
    step_bias,
    decay_log,
    skip_gain,
    norm_gain,
):
    z_at = lax.axis_index("zh") * 4 + lax.axis_index("zl")
    at = jnp.stack([z_at, *(lax.axis_index(name) for name in ("core", "xb", "xa", "y"))])
    block = lax.all_to_all(
        cut_call(lengths, projection),
        ("xa", "xb", "core", "y"),
        split_axis=0,
        concat_axis=0,
        tiled=True,
    ).reshape(DEPTH, SENT)
    own = norm_call(at, hidden, input_gain.reshape(1, D))
    own_x = swap_x(own)
    other = swap_core(own)
    block, own = lax.optimization_barrier((block, own))

    together = lax.optimization_barrier
    w0, lengths_all = pack_call(block)
    w1, w7 = from_z(w0, 1), from_z(w0, -1)
    w1, w7, other = together((w1, w7, other))
    w2, w6 = from_z(w1, 1), from_z(w7, -1)
    w2, w6, own_x = together((w2, w6, own_x))
    far = swap_core(own_x)
    w3, w5 = from_z(w2, 1), from_z(w6, -1)
    early = [w0, w1, w7, w2, w6]
    near = pair_call([own, other], early, 0, None, "near")[0]
    away = pair_call([own_x, far], early, 0, None, "away")[0]
    w3, w5, near, away = together((w3, w5, near, away))
    a4, b4 = from_z(w3[:HALF], 1), from_z(w5[HALF:], -1)
    late = [w3, w5]
    near, near_last = pair_call([own, other], late, DZ_AT[3] * DEPTH, near, "near_late")
    away, away_last = pair_call([own_x, far], late, DZ_AT[3] * DEPTH, away, "away_late")
    x_cols, bc_own, steps, gate = last_call(
        at, (near_last, away_last), (near, away), (a4, b4), bc_kernel, bc_offset
    )
    bc_other = swap_core(bc_own)
    arguments = (
        at,
        skip_gain,
        step_bias,
        decay_log,
        lengths_all,
        gate,
        x_cols,
        bc_own,
        bc_other,
        steps,
        x_kernel,
        x_offset.reshape(1, 4 * QUARTER),
    )
    far_out, x_out = core_call((3, 2), *arguments)
    arguments, far_out, x_out = together((arguments, far_out, x_out))
    got_far, got_x = swap_both(far_out), swap_x(x_out)
    (other_out,) = core_call((1,), *arguments)
    arguments, other_out = together((arguments, other_out))
    got_other = swap_core(other_out)
    gated, state = core_call((0,), *arguments)
    mixer_out, final_state = final_call(
        at, lengths, gated, state, (got_far, got_x, got_other), norm_gain.reshape(1, 4 * QUARTER)
    )
    return mixer_out, final_state.reshape(1, 4 * HEADS, QUARTER // HEADS, NST)


def solution(mesh):
    names = ("xa", "xb", "zl", "core", "zh", "y")
    fine = Mesh(mesh.devices.reshape(2, 2, 4, 2, 2, 8), names)
    replica = names[:5]
    in_specs = (
        P(replica, None),
        P(replica),
        P(names, None),
        P(),
        P(None, "y"),
        P("y"),
        P(None, None, "y"),
        P(None, "y"),
        P("y"),
        P("y"),
        P("y"),
        P("y"),
    )
    out_specs = (P(replica, "y"), P(replica, "y", None, None))
    return jax.shard_map(
        on_device, mesh=fine, in_specs=in_specs, out_specs=out_specs, check_vma=False
    )
```

```python
import functools

import jax
import jax.numpy as jnp
from jax import lax
from jax.experimental import pallas as pl
from jax.experimental.pallas import tpu as pltpu
from jax.sharding import Mesh, PartitionSpec as P

EPSILON = 1e-05
F32 = jnp.float32
BF16 = jnp.bfloat16

TOK = 256
D = 4096
QUARTER = 256
NST = 128
HEADS = 4
XC = QUARTER + NST
COLS = XC + QUARTER
WIDE = XC + 128
HALF = 256
DEPTH = 2 * HALF
PACKED = DEPTH + 16
SENT = 768
DZ_ORDER = (0, 1, 7, 2, 6, 3, 5, 4)
DZ_AT = {dz: at for at, dz in enumerate(DZ_ORDER)}

VMEM = pl.BlockSpec(memory_space=pltpu.VMEM)
SMEM = pl.BlockSpec(memory_space=pltpu.SMEM)


def params(mib):
    return pltpu.CompilerParams(vmem_limit_bytes=mib << 20)


def cost(flops, nbytes):
    return pl.CostEstimate(flops=flops, bytes_accessed=nbytes, transcendentals=0)


def silu(value):
    return value * jax.nn.sigmoid(value)


def norm_kernel(at_ref, hidden_ref, gain_ref, out_ref, scale_ref):
    z_at = at_ref[0]
    for rows in range(0, TOK, 32):
        wide = hidden_ref[rows : rows + 32, :].astype(F32)
        mean = jnp.sum(wide * wide, axis=1, keepdims=True) * (1.0 / D)
        scale_ref[rows : rows + 32, :] = jnp.broadcast_to(lax.rsqrt(mean + EPSILON), (32, 128))
    low = lax.broadcasted_iota(jnp.int32, (TOK, 128), 1) < 64
    scale = scale_ref[...]
    for dz in range(4):
        zs = lax.rem(z_at + dz, 8)
        zl = lax.rem(zs, 4)
        here_first = zs < 4
        here = DZ_AT[dz] * DEPTH
        there = DZ_AT[dz + 4] * DEPTH
        here_at = pl.multiple_of(jnp.where(here_first, here, there), 128)
        there_at = pl.multiple_of(jnp.where(here_first, there, here), 128)
        for part in range(4):
            base = pl.multiple_of((part * 4 + zl) * 256, 256)
            second_at = pl.multiple_of(base + 128, 128)
            first = hidden_ref[:, pl.ds(base, 128)].astype(F32) * scale * gain_ref[:, pl.ds(base, 128)]
            second = (
                hidden_ref[:, pl.ds(second_at, 128)].astype(F32)
                * scale
                * gain_ref[:, pl.ds(second_at, 128)]
            )
            low_half = jnp.where(low, first, pltpu.roll(second, 64, 1)).astype(BF16)
            high_half = jnp.where(low, pltpu.roll(first, 64, 1), second).astype(BF16)
            out_ref[:, pl.ds(pl.multiple_of(here_at + part * 128, 128), 128)] = low_half
            out_ref[:, pl.ds(pl.multiple_of(there_at + part * 128, 128), 128)] = high_half


def norm_call(at, hidden, gain):
    return pl.pallas_call(
        norm_kernel,
        out_shape=jax.ShapeDtypeStruct((TOK, D), BF16),
        in_specs=[SMEM, VMEM, VMEM],
        out_specs=VMEM,
        scratch_shapes=[pltpu.VMEM((TOK, 128), F32)],
        compiler_params=params(32),
        cost_estimate=cost(TOK * D * 8, TOK * D * 4),
        name="norm",
    )(at, hidden, gain)


def cut_kernel(length_ref, rows_ref, out_ref):
    inner = 32 * QUARTER
    lane = lax.broadcasted_iota(jnp.int32, (8, 128), 1)
    length = length_ref[0].astype(F32)
    steps = rows_ref[:, 2 * inner + 2048 :].astype(F32)
    for to in range(32):
        group, y = to // 8, to % 8
        units = y * 4 * QUARTER + group * QUARTER
        bc = 2 * inner + (group % 2) * 1024 + y * NST
        at = y * 16 + group * HEADS
        mine = steps if at == 0 else pltpu.roll(steps, 128 - at, 1)
        tail = jnp.where(lane < HEADS, mine, jnp.where(lane == HEADS, length, 0.0))
        for side in (to, to + 32):
            out_ref[side, :, :QUARTER] = rows_ref[:, inner + units : inner + units + QUARTER]
            out_ref[side, :, QUARTER:XC] = rows_ref[:, bc : bc + NST]
            out_ref[side, :, XC:COLS] = rows_ref[:, units : units + QUARTER]
            out_ref[side, :, COLS:] = tail.astype(BF16)


def cut_call(length, rows):
    return pl.pallas_call(
        cut_kernel,
        out_shape=jax.ShapeDtypeStruct((64, 8, SENT), BF16),
        in_specs=[SMEM, VMEM],
        out_specs=VMEM,
        compiler_params=params(32),
        cost_estimate=cost(1000, 1000),
        name="cut",
    )(length, rows)


def pack_kernel(block_ref, out_ref, lengths_ref):
    out_ref[:DEPTH, :] = block_ref[:, :COLS]
    tail = block_ref[:, COLS:].astype(F32).T
    row = lax.broadcasted_iota(jnp.int32, (8, HALF), 0)
    halves = [jnp.where(row < HEADS, tail[:8, at : at + HALF], 0.0) for at in (0, HALF)]
    out_ref[DEPTH:, :HALF] = jnp.concatenate(halves, axis=0).astype(BF16)
    out_ref[DEPTH:, HALF:] = jnp.zeros((16, COLS - HALF), BF16)
    lengths_ref[...] = tail[:8]


def pack_call(block):
    return pl.pallas_call(
        pack_kernel,
        out_shape=(
            jax.ShapeDtypeStruct((PACKED, COLS), BF16),
            jax.ShapeDtypeStruct((8, DEPTH), F32),
        ),
        in_specs=[VMEM],
        out_specs=(VMEM, VMEM),
        compiler_params=params(32),
        cost_estimate=cost(1000, 1000),
        name="pack",
    )(block)


def step_columns(tile):
    wide = jnp.concatenate([tile.astype(F32), jnp.zeros((112, HALF), F32)], axis=0).T
    return [wide.astype(BF16), pltpu.roll(wide, 120, 1).astype(BF16)]


def products(hidden_refs, weight_refs, first, use):
    rows = [ref[: ref.shape[0] // HALF * HALF, :] for ref in weight_refs]
    steps = []
    for ref in weight_refs:
        if ref.shape[0] % HALF:
            steps += step_columns(ref[ref.shape[0] - 16 :, :HALF])
    rows = jnp.concatenate(rows, axis=0)
    steps = jnp.concatenate(steps, axis=0)
    right = jnp.concatenate([rows[:, :XC], steps, rows[:, XC:]], axis=1)
    for seq, ref in enumerate(hidden_refs):
        left = ref[:, first : first + right.shape[0]]
        use(seq, jnp.dot(left, right, preferred_element_type=F32))


def pair_kernel(count, first, has_total, *refs):
    weight_refs = refs[2 : 2 + count]
    out_ref = refs[-2 if has_total else -1]

    def use(seq, part):
        rows = pl.ds(seq * TOK, TOK)
        out_ref[rows, :] = part + refs[2 + count][rows, :] if has_total else part
        if has_total:
            refs[-1][rows, :] = refs[seq][:, DZ_AT[4] * DEPTH :]

    products(refs[:2], weight_refs, first, use)


def pair_call(hiddens, weights, first, total, name):
    operands = [*hiddens, *weights] + ([] if total is None else [total])
    shapes = [jax.ShapeDtypeStruct((2 * TOK, WIDE + QUARTER), F32)]
    if total is not None:
        shapes.append(jax.ShapeDtypeStruct((2 * TOK, DEPTH), BF16))
    return pl.pallas_call(
        functools.partial(pair_kernel, len(weights), first, total is not None),
        out_shape=tuple(shapes),
        in_specs=[VMEM] * len(operands),
        out_specs=(VMEM,) * len(shapes),
        compiler_params=params(48),
        cost_estimate=cost(4 * TOK * DEPTH * len(weights) * (WIDE + QUARTER), 4 * TOK * D),
        name=name,
    )(*operands)


def shifted(value, by):
    row = lax.broadcasted_iota(jnp.int32, value.shape, 0)
    return jnp.where(row < by, 0.0, pltpu.roll(value, by, 0))


def causal_conv(value, taps, offset):
    total = offset + taps[0] * shifted(value, 3)
    total = total + taps[1] * shifted(value, 2)
    total = total + taps[2] * shifted(value, 1)
    return total + taps[3] * value


def last_kernel(count, at_ref, *refs):
    totals, weight_refs = refs[2:4], refs[4 : 4 + count]
    kernel_ref, offset_ref, x_ref, bc_ref, steps_ref, gate_ref = refs[4 + count :]
    core = at_ref[1]
    taps = [kernel_ref[tap, pl.ds(core, 1), :] for tap in range(4)]
    offset = offset_ref[pl.ds(core, 1), :]

    def use(seq, part):
        rows = pl.ds(seq * TOK, TOK)
        part = part + totals[seq // 2][pl.ds(seq % 2 * TOK, TOK), :]
        x_ref[rows, :] = part[:, :QUARTER]
        bc_ref[rows, :] = silu(causal_conv(part[:, QUARTER:XC], taps, offset)).astype(BF16)
        steps_ref[rows, :] = part[:, XC:WIDE]
        gate_ref[rows, :] = silu(part[:, WIDE:])

    hidden_refs = [refs[seq // 2].at[pl.ds(seq % 2 * TOK, TOK), :] for seq in range(4)]
    products(hidden_refs, weight_refs, 0, use)


def last_call(at, hiddens, totals, weights, bc_kernel, bc_offset):
    return pl.pallas_call(
        functools.partial(last_kernel, len(weights)),
        out_shape=(
            jax.ShapeDtypeStruct((4 * TOK, QUARTER), F32),
            jax.ShapeDtypeStruct((4 * TOK, NST), BF16),
            jax.ShapeDtypeStruct((4 * TOK, 128), F32),
            jax.ShapeDtypeStruct((4 * TOK, QUARTER), F32),
        ),
        in_specs=[SMEM] + [VMEM] * (6 + len(weights)),
        out_specs=(VMEM,) * 4,
        compiler_params=params(40),
        cost_estimate=cost(8 * TOK * DEPTH * (WIDE + QUARTER), 8 * TOK * WIDE),
        name="last",
    )(at, *hiddens, *totals, *weights, bc_kernel, bc_offset)


def core_of(seq, refs, out_refs):
    (
        at_ref,
        skip_ref,
        bias_ref,
        decay_ref,
        length_ref,
        gate_ref,
        x_ref,
        bc_own_ref,
        bc_other_ref,
        step_ref,
        x_kernel_ref,
        x_offset_ref,
    ) = refs
    rows = slice(seq * TOK, seq * TOK + TOK)
    turned = slice((seq ^ 1) * TOK, (seq ^ 1) * TOK + TOK)
    core = at_ref[1]
    group = at_ref[2] * 2 + core
    units = pl.ds(pl.multiple_of(group * QUARTER, QUARTER), QUARTER)
    mine = core == 0
    b_act = jnp.where(mine, bc_own_ref[rows, :], bc_other_ref[turned, :])
    c_act = jnp.where(mine, bc_other_ref[turned, :], bc_own_ref[rows, :])
    x_taps = [x_kernel_ref[tap : tap + 1, units] for tap in range(4)]
    x_act = silu(causal_conv(x_ref[rows, :], x_taps, x_offset_ref[:, units])).astype(BF16)
    x_wide = x_act.astype(F32)

    head_at = lax.broadcasted_iota(jnp.int32, (8, TOK), 0)
    bias = jnp.zeros((8, TOK), F32)
    decay = jnp.zeros((8, TOK), F32)
    for head in range(HEADS):
        bias = jnp.where(head_at == head, bias_ref[group * HEADS + head], bias)
        decay = jnp.where(head_at == head, decay_ref[group * HEADS + head], decay)
    holder = ((at_ref[3] * 4 + jnp.bitwise_xor(group, seq)) * 8 + at_ref[4]) * 8
    lane = lax.broadcasted_iota(jnp.int32, (1, DEPTH), 1)
    length = jnp.sum(jnp.where(lane == holder, length_ref[HEADS : HEADS + 1, :], 0.0))
    live = lax.broadcasted_iota(jnp.int32, (8, TOK), 1).astype(F32) < length
    raw = step_ref[rows, :].T[:8] + bias
    soft = jnp.maximum(raw, 0.0) + jnp.log1p(jnp.exp(-jnp.abs(raw)))
    step = jnp.where(live, soft, 0.0)
    ends = -jnp.exp(decay) * step
    row = lax.broadcasted_iota(jnp.int32, (TOK, TOK), 0)
    col = lax.broadcasted_iota(jnp.int32, (TOK, TOK), 1)
    ones = jnp.where(row <= col, 1.0, 0.0).astype(BF16)
    high = ends.astype(BF16)
    rest = ends - high.astype(F32)
    middle = rest.astype(BF16)
    lowest = (rest - middle.astype(F32)).astype(BF16)
    split = jnp.concatenate([part.astype(F32) for part in (high, middle, lowest)], axis=0)
    summed = jnp.dot(split.astype(BF16), ones, preferred_element_type=F32)
    sums = summed[:8] + summed[8:16] + summed[16:]
    left_over = jnp.exp(sums[:, TOK - 1 :] - sums) * step
    packed = jnp.concatenate([sums, left_over, jnp.zeros((112, TOK), F32)], axis=0)
    columns = packed.T

    scores = lax.dot_general(c_act, b_act, (((1,), (1,)), ((), ())), preferred_element_type=F32)
    half = TOK // 2
    causal = (row >= col)[:half, :half]
    low = lax.broadcasted_iota(jnp.int32, (TOK, 128), 1) < 64
    outs, weighted = [], []
    for pair in range(HEADS // 2):
        lanes = slice(pair * 128, pair * 128 + 128)
        halves = []
        for head in (2 * pair, 2 * pair + 1):
            def quarter(t_at, u_at):
                t, u = slice(t_at, t_at + half), slice(u_at, u_at + half)
                spread = columns[t, head : head + 1] - sums[head : head + 1, u]
                if t_at == u_at:
                    spread = jnp.where(causal, spread, -1e30)
                return (scores[t, u] * jnp.exp(spread) * step[head : head + 1, u]).astype(BF16)

            first = jnp.dot(quarter(0, 0), x_act[:half, lanes], preferred_element_type=F32)
            mixing = jnp.concatenate([quarter(half, 0), quarter(half, half)], axis=1)
            second = jnp.dot(mixing, x_act[:, lanes], preferred_element_type=F32)
            halves.append(jnp.concatenate([first, second], axis=0))
        skip = jnp.where(
            low[:1], skip_ref[group * HEADS + 2 * pair], skip_ref[group * HEADS + 2 * pair + 1]
        )
        outs.append(jnp.where(low, halves[0], halves[1]) + skip * x_wide[:, lanes])
        at = 8 + 2 * pair
        weighted.append(
            x_wide[:, lanes] * jnp.where(low, columns[:, at : at + 1], columns[:, at + 1 : at + 2])
        )
    gated = jnp.concatenate(outs, axis=1) * gate_ref[rows, :]
    spread_x = jnp.concatenate(weighted, axis=1)
    state = jnp.dot(spread_x.T.astype(BF16), b_act, preferred_element_type=F32)
    if seq == 0:
        out_refs[0][...] = gated
        out_refs[1][...] = state
    else:
        out_refs[0][:, :QUARTER] = gated.astype(BF16)
        out_refs[0][:, QUARTER:] = state.astype(BF16)


def core_kernel(seqs, *refs):
    for at, seq in enumerate(seqs):
        core_of(seq, refs[:12], refs[12 + at :])


def core_call(seqs, *operands):
    shapes = [jax.ShapeDtypeStruct((TOK, QUARTER + NST), BF16) for seq in seqs if seq]
    if seqs[-1] == 0:
        shapes += [
            jax.ShapeDtypeStruct((TOK, QUARTER), F32),
            jax.ShapeDtypeStruct((QUARTER, NST), F32),
        ]
    return pl.pallas_call(
        functools.partial(core_kernel, seqs),
        out_shape=tuple(shapes),
        in_specs=[SMEM] * 4 + [VMEM] * 8,
        out_specs=(VMEM,) * len(shapes),
        compiler_params=params(40),
        cost_estimate=cost(len(seqs) * 8 * TOK * TOK * 200, len(seqs) * 8 * TOK * QUARTER),
        name="core" + "".join(str(seq) for seq in seqs),
    )(*operands)


def final_kernel(at_ref, length_ref, own_ref, state_ref, a_ref, b_ref, c_ref, gain_ref, out_ref, final_ref):
    group = at_ref[2] * 2 + at_ref[1]
    own = own_ref[...]
    squares = jnp.sum(own * own, axis=1, keepdims=True)
    parts = [(0, own)]
    for flip, ref in ((1, a_ref), (2, b_ref), (3, c_ref)):
        part = ref[:, :QUARTER].astype(F32)
        squares = squares + jnp.sum(part * part, axis=1, keepdims=True)
        parts.append((flip, part))
    live = lax.broadcasted_iota(jnp.int32, (TOK, 1), 0) < length_ref[0]
    scale = jnp.where(live, lax.rsqrt(squares * (1.0 / (4 * QUARTER)) + EPSILON), 0.0)
    for flip, part in parts:
        at = pl.ds(pl.multiple_of(jnp.bitwise_xor(group, flip) * QUARTER, QUARTER), QUARTER)
        out_ref[:, at] = (part * scale * gain_ref[:, at]).astype(BF16)
        if flip == 0:
            final_ref[at, :] = state_ref[...]
        else:
            final_ref[at, :] = (a_ref, b_ref, c_ref)[flip - 1][:, QUARTER:].astype(F32)


def final_call(at, length, own, state, got, gain):
    return pl.pallas_call(
        final_kernel,
        out_shape=(
            jax.ShapeDtypeStruct((TOK, 4 * QUARTER), BF16),
            jax.ShapeDtypeStruct((4 * QUARTER, NST), F32),
        ),
        in_specs=[SMEM, SMEM] + [VMEM] * 6,
        out_specs=(VMEM, VMEM),
        compiler_params=params(32),
        cost_estimate=cost(TOK * QUARTER * 40, TOK * QUARTER * 32),
        name="gated_norm",
    )(at, length, own, state, *got, gain)


def from_z(value, distance):
    flat = lambda z: (z % 4) * 2 + z // 4
    return lax.ppermute(
        value, ("zl", "zh"), [(flat((i + distance) % 8), flat(i)) for i in range(8)]
    )


def swap_core(value):
    return lax.ppermute(value, "core", [(0, 1), (1, 0)])


def swap_x(value):
    return lax.ppermute(value, "xb", [(0, 1), (1, 0)])


def swap_both(value):
    return lax.ppermute(value, ("xb", "core"), [(0, 3), (1, 2), (2, 1), (3, 0)])


def on_device(
    hidden,
    lengths,
    projection,
    input_gain,
    x_kernel,
    x_offset,
    bc_kernel,
    bc_offset,
    step_bias,
    decay_log,
    skip_gain,
    norm_gain,
):
    z_at = lax.axis_index("zh") * 4 + lax.axis_index("zl")
    at = jnp.stack([z_at, *(lax.axis_index(name) for name in ("core", "xb", "xa", "y"))])
    block = lax.all_to_all(
        cut_call(lengths, projection),
        ("xa", "xb", "core", "y"),
        split_axis=0,
        concat_axis=0,
        tiled=True,
    ).reshape(DEPTH, SENT)
    own = norm_call(at, hidden, input_gain.reshape(1, D))
    own_x = swap_x(own)
    other = swap_core(own)
    block, own = lax.optimization_barrier((block, own))

    together = lax.optimization_barrier
    w0, lengths_all = pack_call(block)
    w1, w7 = from_z(w0, 1), from_z(w0, -1)
    w1, w7, other = together((w1, w7, other))
    w2, w6 = from_z(w1, 1), from_z(w7, -1)
    w2, w6, own_x = together((w2, w6, own_x))
    far = swap_core(own_x)
    w3, w5 = from_z(w2, 1), from_z(w6, -1)
    early = [w0, w1, w7, w2, w6]
    near = pair_call([own, other], early, 0, None, "near")[0]
    away = pair_call([own_x, far], early, 0, None, "away")[0]
    w3, w5, near, away = together((w3, w5, near, away))
    a4, b4 = from_z(w3[:HALF], 1), from_z(w5[HALF:], -1)
    late = [w3, w5]
    near, near_last = pair_call([own, other], late, DZ_AT[3] * DEPTH, near, "near_late")
    away, away_last = pair_call([own_x, far], late, DZ_AT[3] * DEPTH, away, "away_late")
    x_cols, bc_own, steps, gate = last_call(
        at, (near_last, away_last), (near, away), (a4, b4), bc_kernel, bc_offset
    )
    bc_other = swap_core(bc_own)
    arguments = (
        at,
        skip_gain,
        step_bias,
        decay_log,
        lengths_all,
        gate,
        x_cols,
        bc_own,
        bc_other,
        steps,
        x_kernel,
        x_offset.reshape(1, 4 * QUARTER),
    )
    got_far = swap_both(core_call((3,), *arguments)[0])
    got_x = swap_x(core_call((2,), *arguments)[0])
    got_other = swap_core(core_call((1,), *arguments)[0])
    gated, state = core_call((0,), *arguments)
    mixer_out, final_state = final_call(
        at, lengths, gated, state, (got_other, got_x, got_far), norm_gain.reshape(1, 4 * QUARTER)
    )
    return mixer_out, final_state.reshape(1, 4 * HEADS, QUARTER // HEADS, NST)


def solution(mesh):
    names = ("xa", "xb", "zl", "core", "zh", "y")
    fine = Mesh(mesh.devices.reshape(2, 2, 4, 2, 2, 8), names)
    replica = names[:5]
    in_specs = (
        P(replica, None),
        P(replica),
        P(names, None),
        P(),
        P(None, "y"),
        P("y"),
        P(None, None, "y"),
        P(None, "y"),
        P("y"),
        P("y"),
        P("y"),
        P("y"),
    )
    out_specs = (P(replica, "y"), P(replica, "y", None, None))
    return jax.shard_map(
        on_device, mesh=fine, in_specs=in_specs, out_specs=out_specs, check_vma=False
    )
```

```python
import functools

import jax
import jax.numpy as jnp
from jax import lax
from jax.experimental import pallas as pl
from jax.experimental.pallas import tpu as pltpu
from jax.sharding import Mesh, PartitionSpec as P

EPSILON = 1e-05
F32 = jnp.float32
BF16 = jnp.bfloat16

TOK = 256
D = 4096
QUARTER = 256
NST = 128
HEADS = 4
XC = QUARTER + NST
COLS = XC + QUARTER
WIDE = XC + 128
HALF = 256
DEPTH = 2 * HALF
PACKED = DEPTH + 16
SENT = 768
DZ_ORDER = (0, 1, 7, 2, 6, 3, 5, 4)
DZ_AT = {dz: at for at, dz in enumerate(DZ_ORDER)}

VMEM = pl.BlockSpec(memory_space=pltpu.VMEM)
SMEM = pl.BlockSpec(memory_space=pltpu.SMEM)


def params(mib):
    return pltpu.CompilerParams(vmem_limit_bytes=mib << 20)


def cost(flops, nbytes):
    return pl.CostEstimate(flops=flops, bytes_accessed=nbytes, transcendentals=0)


def silu(value):
    return value * jax.nn.sigmoid(value)


def norm_kernel(at_ref, hidden_ref, gain_ref, out_ref, scale_ref):
    z_at = at_ref[0]
    for rows in range(0, TOK, 32):
        wide = hidden_ref[rows : rows + 32, :].astype(F32)
        mean = jnp.sum(wide * wide, axis=1, keepdims=True) * (1.0 / D)
        scale_ref[rows : rows + 32, :] = jnp.broadcast_to(lax.rsqrt(mean + EPSILON), (32, 128))
    low = lax.broadcasted_iota(jnp.int32, (TOK, 128), 1) < 64
    scale = scale_ref[...]
    for dz in range(4):
        zs = lax.rem(z_at + dz, 8)
        zl = lax.rem(zs, 4)
        here_first = zs < 4
        here = DZ_AT[dz] * DEPTH
        there = DZ_AT[dz + 4] * DEPTH
        here_at = pl.multiple_of(jnp.where(here_first, here, there), 128)
        there_at = pl.multiple_of(jnp.where(here_first, there, here), 128)
        for part in range(4):
            base = pl.multiple_of((part * 4 + zl) * 256, 256)
            second_at = pl.multiple_of(base + 128, 128)
            first = hidden_ref[:, pl.ds(base, 128)].astype(F32) * scale * gain_ref[:, pl.ds(base, 128)]
            second = (
                hidden_ref[:, pl.ds(second_at, 128)].astype(F32)
                * scale
                * gain_ref[:, pl.ds(second_at, 128)]
            )
            low_half = jnp.where(low, first, pltpu.roll(second, 64, 1)).astype(BF16)
            high_half = jnp.where(low, pltpu.roll(first, 64, 1), second).astype(BF16)
            out_ref[:, pl.ds(pl.multiple_of(here_at + part * 128, 128), 128)] = low_half
            out_ref[:, pl.ds(pl.multiple_of(there_at + part * 128, 128), 128)] = high_half


def norm_call(at, hidden, gain):
    return pl.pallas_call(
        norm_kernel,
        out_shape=jax.ShapeDtypeStruct((TOK, D), BF16),
        in_specs=[SMEM, VMEM, VMEM],
        out_specs=VMEM,
        scratch_shapes=[pltpu.VMEM((TOK, 128), F32)],
        compiler_params=params(32),
        cost_estimate=cost(TOK * D * 8, TOK * D * 4),
        name="norm",
    )(at, hidden, gain)


def cut_kernel(length_ref, rows_ref, out_ref):
    inner = 32 * QUARTER
    lane = lax.broadcasted_iota(jnp.int32, (8, 128), 1)
    length = length_ref[0].astype(F32)
    steps = rows_ref[:, 2 * inner + 2048 :].astype(F32)
    for to in range(32):
        group, y = to // 8, to % 8
        units = y * 4 * QUARTER + group * QUARTER
        bc = 2 * inner + (group % 2) * 1024 + y * NST
        at = y * 16 + group * HEADS
        mine = steps if at == 0 else pltpu.roll(steps, 128 - at, 1)
        tail = jnp.where(lane < HEADS, mine, jnp.where(lane == HEADS, length, 0.0))
        for side in (to, to + 32):
            out_ref[side, :, :QUARTER] = rows_ref[:, inner + units : inner + units + QUARTER]
            out_ref[side, :, QUARTER:XC] = rows_ref[:, bc : bc + NST]
            out_ref[side, :, XC:COLS] = rows_ref[:, units : units + QUARTER]
            out_ref[side, :, COLS:] = tail.astype(BF16)


def cut_call(length, rows):
    return pl.pallas_call(
        cut_kernel,
        out_shape=jax.ShapeDtypeStruct((64, 8, SENT), BF16),
        in_specs=[SMEM, VMEM],
        out_specs=VMEM,
        compiler_params=params(32),
        cost_estimate=cost(1000, 1000),
        name="cut",
    )(length, rows)


def pack_kernel(block_ref, out_ref, lengths_ref):
    out_ref[:DEPTH, :] = block_ref[:, :COLS]
    tail = block_ref[:, COLS:].astype(F32).T
    row = lax.broadcasted_iota(jnp.int32, (8, HALF), 0)
    halves = [jnp.where(row < HEADS, tail[:8, at : at + HALF], 0.0) for at in (0, HALF)]
    out_ref[DEPTH:, :HALF] = jnp.concatenate(halves, axis=0).astype(BF16)
    out_ref[DEPTH:, HALF:] = jnp.zeros((16, COLS - HALF), BF16)
    lengths_ref[...] = tail[:8]


def pack_call(block):
    return pl.pallas_call(
        pack_kernel,
        out_shape=(
            jax.ShapeDtypeStruct((PACKED, COLS), BF16),
            jax.ShapeDtypeStruct((8, DEPTH), F32),
        ),
        in_specs=[VMEM],
        out_specs=(VMEM, VMEM),
        compiler_params=params(32),
        cost_estimate=cost(1000, 1000),
        name="pack",
    )(block)


def step_columns(tile):
    wide = jnp.concatenate([tile.astype(F32), jnp.zeros((112, HALF), F32)], axis=0).T
    return [wide.astype(BF16), pltpu.roll(wide, 120, 1).astype(BF16)]


def products(hidden_refs, weight_refs, first, use):
    rows = [ref[: ref.shape[0] // HALF * HALF, :] for ref in weight_refs]
    steps = []
    for ref in weight_refs:
        if ref.shape[0] % HALF:
            steps += step_columns(ref[ref.shape[0] - 16 :, :HALF])
    rows = jnp.concatenate(rows, axis=0)
    steps = jnp.concatenate(steps, axis=0)
    right = jnp.concatenate([rows[:, :XC], steps, rows[:, XC:]], axis=1)
    for seq, ref in enumerate(hidden_refs):
        left = ref[:, first : first + right.shape[0]]
        use(seq, jnp.dot(left, right, preferred_element_type=F32))


def pair_kernel(count, first, has_total, *refs):
    weight_refs = refs[2 : 2 + count]
    out_ref = refs[-2 if has_total else -1]

    def use(seq, part):
        rows = pl.ds(seq * TOK, TOK)
        out_ref[rows, :] = part + refs[2 + count][rows, :] if has_total else part
        if has_total:
            refs[-1][rows, :] = refs[seq][:, DZ_AT[4] * DEPTH :]

    products(refs[:2], weight_refs, first, use)


def pair_call(hiddens, weights, first, total, name):
    operands = [*hiddens, *weights] + ([] if total is None else [total])
    shapes = [jax.ShapeDtypeStruct((2 * TOK, WIDE + QUARTER), F32)]
    if total is not None:
        shapes.append(jax.ShapeDtypeStruct((2 * TOK, DEPTH), BF16))
    return pl.pallas_call(
        functools.partial(pair_kernel, len(weights), first, total is not None),
        out_shape=tuple(shapes),
        in_specs=[VMEM] * len(operands),
        out_specs=(VMEM,) * len(shapes),
        compiler_params=params(48),
        cost_estimate=cost(4 * TOK * DEPTH * len(weights) * (WIDE + QUARTER), 4 * TOK * D),
        name=name,
    )(*operands)


def shifted(value, by):
    row = lax.broadcasted_iota(jnp.int32, value.shape, 0)
    return jnp.where(row < by, 0.0, pltpu.roll(value, by, 0))


def causal_conv(value, taps, offset):
    total = offset + taps[0] * shifted(value, 3)
    total = total + taps[1] * shifted(value, 2)
    total = total + taps[2] * shifted(value, 1)
    return total + taps[3] * value


def last_kernel(count, at_ref, *refs):
    totals, weight_refs = refs[2:4], refs[4 : 4 + count]
    kernel_ref, offset_ref, x_ref, bc_ref, steps_ref, gate_ref = refs[4 + count :]
    core = at_ref[1]
    taps = [kernel_ref[tap, pl.ds(core, 1), :] for tap in range(4)]
    offset = offset_ref[pl.ds(core, 1), :]

    def use(seq, part):
        rows = pl.ds(seq * TOK, TOK)
        part = part + totals[seq // 2][pl.ds(seq % 2 * TOK, TOK), :]
        x_ref[rows, :] = part[:, :QUARTER]
        bc_ref[rows, :] = silu(causal_conv(part[:, QUARTER:XC], taps, offset)).astype(BF16)
        steps_ref[rows, :] = part[:, XC:WIDE]
        gate_ref[rows, :] = silu(part[:, WIDE:])

    hidden_refs = [refs[seq // 2].at[pl.ds(seq % 2 * TOK, TOK), :] for seq in range(4)]
    products(hidden_refs, weight_refs, 0, use)


def last_call(at, hiddens, totals, weights, bc_kernel, bc_offset):
    return pl.pallas_call(
        functools.partial(last_kernel, len(weights)),
        out_shape=(
            jax.ShapeDtypeStruct((4 * TOK, QUARTER), F32),
            jax.ShapeDtypeStruct((4 * TOK, NST), BF16),
            jax.ShapeDtypeStruct((4 * TOK, 128), F32),
            jax.ShapeDtypeStruct((4 * TOK, QUARTER), F32),
        ),
        in_specs=[SMEM] + [VMEM] * (6 + len(weights)),
        out_specs=(VMEM,) * 4,
        compiler_params=params(40),
        cost_estimate=cost(8 * TOK * DEPTH * (WIDE + QUARTER), 8 * TOK * WIDE),
        name="last",
    )(at, *hiddens, *totals, *weights, bc_kernel, bc_offset)


def core_of(seq, refs, out_refs):
    (
        at_ref,
        skip_ref,
        bias_ref,
        decay_ref,
        length_ref,
        gate_ref,
        x_ref,
        bc_own_ref,
        bc_other_ref,
        step_ref,
        x_kernel_ref,
        x_offset_ref,
    ) = refs
    rows = slice(seq * TOK, seq * TOK + TOK)
    turned = slice((seq ^ 1) * TOK, (seq ^ 1) * TOK + TOK)
    core = at_ref[1]
    group = at_ref[2] * 2 + core
    units = pl.ds(pl.multiple_of(group * QUARTER, QUARTER), QUARTER)
    mine = core == 0
    b_act = jnp.where(mine, bc_own_ref[rows, :], bc_other_ref[turned, :])
    c_act = jnp.where(mine, bc_other_ref[turned, :], bc_own_ref[rows, :])
    x_taps = [x_kernel_ref[tap : tap + 1, units] for tap in range(4)]
    x_act = silu(causal_conv(x_ref[rows, :], x_taps, x_offset_ref[:, units])).astype(BF16)
    x_wide = x_act.astype(F32)

    head_at = lax.broadcasted_iota(jnp.int32, (8, TOK), 0)
    bias = jnp.zeros((8, TOK), F32)
    decay = jnp.zeros((8, TOK), F32)
    for head in range(HEADS):
        bias = jnp.where(head_at == head, bias_ref[group * HEADS + head], bias)
        decay = jnp.where(head_at == head, decay_ref[group * HEADS + head], decay)
    holder = ((at_ref[3] * 4 + jnp.bitwise_xor(group, seq)) * 8 + at_ref[4]) * 8
    lane = lax.broadcasted_iota(jnp.int32, (1, DEPTH), 1)
    length = jnp.sum(jnp.where(lane == holder, length_ref[HEADS : HEADS + 1, :], 0.0))
    live = lax.broadcasted_iota(jnp.int32, (8, TOK), 1).astype(F32) < length
    raw = step_ref[rows, :].T[:8] + bias
    soft = jnp.maximum(raw, 0.0) + jnp.log1p(jnp.exp(-jnp.abs(raw)))
    step = jnp.where(live, soft, 0.0)
    ends = -jnp.exp(decay) * step
    row = lax.broadcasted_iota(jnp.int32, (TOK, TOK), 0)
    col = lax.broadcasted_iota(jnp.int32, (TOK, TOK), 1)
    ones = jnp.where(row <= col, 1.0, 0.0).astype(BF16)
    high = ends.astype(BF16)
    rest = ends - high.astype(F32)
    middle = rest.astype(BF16)
    lowest = (rest - middle.astype(F32)).astype(BF16)
    split = jnp.concatenate([part.astype(F32) for part in (high, middle, lowest)], axis=0)
    summed = jnp.dot(split.astype(BF16), ones, preferred_element_type=F32)
    sums = summed[:8] + summed[8:16] + summed[16:]
    left_over = jnp.exp(sums[:, TOK - 1 :] - sums) * step
    packed = jnp.concatenate([sums, left_over, jnp.zeros((112, TOK), F32)], axis=0)
    columns = packed.T

    scores = lax.dot_general(c_act, b_act, (((1,), (1,)), ((), ())), preferred_element_type=F32)
    half = TOK // 2
    causal = (row >= col)[:half, :half]
    low = lax.broadcasted_iota(jnp.int32, (TOK, 128), 1) < 64
    outs, weighted = [], []
    for pair in range(HEADS // 2):
        lanes = slice(pair * 128, pair * 128 + 128)
        halves = []
        for head in (2 * pair, 2 * pair + 1):
            def quarter(t_at, u_at):
                t, u = slice(t_at, t_at + half), slice(u_at, u_at + half)
                spread = columns[t, head : head + 1] - sums[head : head + 1, u]
                if t_at == u_at:
                    spread = jnp.where(causal, spread, -1e30)
                return (scores[t, u] * jnp.exp(spread) * step[head : head + 1, u]).astype(BF16)

            first = jnp.dot(quarter(0, 0), x_act[:half, lanes], preferred_element_type=F32)
            mixing = jnp.concatenate([quarter(half, 0), quarter(half, half)], axis=1)
            second = jnp.dot(mixing, x_act[:, lanes], preferred_element_type=F32)
            halves.append(jnp.concatenate([first, second], axis=0))
        skip = jnp.where(
            low[:1], skip_ref[group * HEADS + 2 * pair], skip_ref[group * HEADS + 2 * pair + 1]
        )
        outs.append(jnp.where(low, halves[0], halves[1]) + skip * x_wide[:, lanes])
        at = 8 + 2 * pair
        weighted.append(
            x_wide[:, lanes] * jnp.where(low, columns[:, at : at + 1], columns[:, at + 1 : at + 2])
        )
    gated = jnp.concatenate(outs, axis=1) * gate_ref[rows, :]
    spread_x = jnp.concatenate(weighted, axis=1)
    state = jnp.dot(spread_x.T.astype(BF16), b_act, preferred_element_type=F32)
    if seq == 0:
        out_refs[0][...] = gated
        out_refs[1][...] = state
    else:
        out_refs[0][:, :QUARTER] = gated.astype(BF16)
        out_refs[0][:, QUARTER:] = state.astype(BF16)


def core_kernel(seqs, *refs):
    for at, seq in enumerate(seqs):
        core_of(seq, refs[:12], refs[12 + at :])


def core_call(seqs, *operands):
    shapes = [jax.ShapeDtypeStruct((TOK, QUARTER + NST), BF16) for seq in seqs if seq]
    if seqs[-1] == 0:
        shapes += [
            jax.ShapeDtypeStruct((TOK, QUARTER), F32),
            jax.ShapeDtypeStruct((QUARTER, NST), F32),
        ]
    return pl.pallas_call(
        functools.partial(core_kernel, seqs),
        out_shape=tuple(shapes),
        in_specs=[SMEM] * 4 + [VMEM] * 8,
        out_specs=(VMEM,) * len(shapes),
        compiler_params=params(40),
        cost_estimate=cost(len(seqs) * 8 * TOK * TOK * 200, len(seqs) * 8 * TOK * QUARTER),
        name="core" + "".join(str(seq) for seq in seqs),
    )(*operands)


def final_kernel(at_ref, length_ref, own_ref, state_ref, a_ref, b_ref, c_ref, gain_ref, out_ref, final_ref):
    group = at_ref[2] * 2 + at_ref[1]
    own = own_ref[...]
    squares = jnp.sum(own * own, axis=1, keepdims=True)
    parts = [(0, own)]
    for flip, ref in ((1, a_ref), (2, b_ref), (3, c_ref)):
        part = ref[:, :QUARTER].astype(F32)
        squares = squares + jnp.sum(part * part, axis=1, keepdims=True)
        parts.append((flip, part))
    live = lax.broadcasted_iota(jnp.int32, (TOK, 1), 0) < length_ref[0]
    scale = jnp.where(live, lax.rsqrt(squares * (1.0 / (4 * QUARTER)) + EPSILON), 0.0)
    for flip, part in parts:
        at = pl.ds(pl.multiple_of(jnp.bitwise_xor(group, flip) * QUARTER, QUARTER), QUARTER)
        out_ref[:, at] = (part * scale * gain_ref[:, at]).astype(BF16)
        if flip == 0:
            final_ref[at, :] = state_ref[...]
        else:
            final_ref[at, :] = (a_ref, b_ref, c_ref)[flip - 1][:, QUARTER:].astype(F32)


def final_call(at, length, own, state, got, gain):
    return pl.pallas_call(
        final_kernel,
        out_shape=(
            jax.ShapeDtypeStruct((TOK, 4 * QUARTER), BF16),
            jax.ShapeDtypeStruct((4 * QUARTER, NST), F32),
        ),
        in_specs=[SMEM, SMEM] + [VMEM] * 6,
        out_specs=(VMEM, VMEM),
        compiler_params=params(32),
        cost_estimate=cost(TOK * QUARTER * 40, TOK * QUARTER * 32),
        name="gated_norm",
    )(at, length, own, state, *got, gain)


def from_z(value, distance):
    flat = lambda z: (z % 4) * 2 + z // 4
    return lax.ppermute(
        value, ("zl", "zh"), [(flat((i + distance) % 8), flat(i)) for i in range(8)]
    )


def swap_core(value):
    return lax.ppermute(value, "core", [(0, 1), (1, 0)])


def swap_x(value):
    return lax.ppermute(value, "xb", [(0, 1), (1, 0)])


def swap_both(value):
    return lax.ppermute(value, ("xb", "core"), [(0, 3), (1, 2), (2, 1), (3, 0)])


def on_device(
    hidden,
    lengths,
    projection,
    input_gain,
    x_kernel,
    x_offset,
    bc_kernel,
    bc_offset,
    step_bias,
    decay_log,
    skip_gain,
    norm_gain,
):
    z_at = lax.axis_index("zh") * 4 + lax.axis_index("zl")
    at = jnp.stack([z_at, *(lax.axis_index(name) for name in ("core", "xb", "xa", "y"))])
    block = lax.all_to_all(
        cut_call(lengths, projection),
        ("xa", "xb", "core", "y"),
        split_axis=0,
        concat_axis=0,
        tiled=True,
    ).reshape(DEPTH, SENT)
    own = norm_call(at, hidden, input_gain.reshape(1, D))
    own_x = swap_x(own)
    other = swap_core(own)
    block, own = lax.optimization_barrier((block, own))

    together = lax.optimization_barrier
    w0, lengths_all = pack_call(block)
    w1, w7 = from_z(w0, 1), from_z(w0, -1)
    w2, w6 = from_z(w1, 1), from_z(w7, -1)
    w2, w6, own_x, other = together((w2, w6, own_x, other))
    far = swap_core(own_x)
    w3, w5 = from_z(w2, 1), from_z(w6, -1)
    early = [w0, w1, w7, w2, w6]
    near = pair_call([own, other], early, 0, None, "near")[0]
    away = pair_call([own_x, far], early, 0, None, "away")[0]
    w3, w5, near, away = together((w3, w5, near, away))
    a4, b4 = from_z(w3[:HALF], 1), from_z(w5[HALF:], -1)
    late = [w3, w5]
    near, near_last = pair_call([own, other], late, DZ_AT[3] * DEPTH, near, "near_late")
    away, away_last = pair_call([own_x, far], late, DZ_AT[3] * DEPTH, away, "away_late")
    x_cols, bc_own, steps, gate = last_call(
        at, (near_last, away_last), (near, away), (a4, b4), bc_kernel, bc_offset
    )
    bc_other = swap_core(bc_own)
    arguments = (
        at,
        skip_gain,
        step_bias,
        decay_log,
        lengths_all,
        gate,
        x_cols,
        bc_own,
        bc_other,
        steps,
        x_kernel,
        x_offset.reshape(1, 4 * QUARTER),
    )
    got_far = swap_both(core_call((3,), *arguments)[0])
    got_x = swap_x(core_call((2,), *arguments)[0])
    got_other = swap_core(core_call((1,), *arguments)[0])
    gated, state = core_call((0,), *arguments)
    mixer_out, final_state = final_call(
        at, lengths, gated, state, (got_other, got_x, got_far), norm_gain.reshape(1, 4 * QUARTER)
    )
    return mixer_out, final_state.reshape(1, 4 * HEADS, QUARTER // HEADS, NST)


def solution(mesh):
    names = ("xa", "xb", "zl", "core", "zh", "y")
    fine = Mesh(mesh.devices.reshape(2, 2, 4, 2, 2, 8), names)
    replica = names[:5]
    in_specs = (
        P(replica, None),
        P(replica),
        P(names, None),
        P(),
        P(None, "y"),
        P("y"),
        P(None, None, "y"),
        P(None, "y"),
        P("y"),
        P("y"),
        P("y"),
        P("y"),
    )
    out_specs = (P(replica, "y"), P(replica, "y", None, None))
    return jax.shard_map(
        on_device, mesh=fine, in_specs=in_specs, out_specs=out_specs, check_vma=False
    )
```
